32 devices in a mesh: inst: 2 (over y), row: 2 (over x), col: 4 (over z), sub: 2 (over core).
Axes of the slice: x: 2, y: 2, z: 4, core: 2. Of those that a mesh axis runs over, the one named last changes fastest.
Arguments:
- a_blocks: bfloat16 [4, 8, 192, 128, 128], P(('inst', 'row'), ('col', 'sub')), parts along dimension 0, may hold values from -0.02734375 to 0.02734375
- block_rows: int32 [4, 8, 192], P(('inst', 'row'), ('col', 'sub')), parts along dimension 0, may hold values from 0 to 31, as said below
- block_cols: int32 [4, 8, 192], P(('inst', 'row'), ('col', 'sub')), parts along dimension 0, may hold values from 0 to 31
- block_count: int32 [4, 8], P(('inst', 'row'), ('col', 'sub')), parts along dimension 0, may hold values from 24 to 192, as said below
- cost: float32 [65536], P(('inst', 'row', 'col', 'sub')), parts along dimension 0, may hold values from -11 to 11
- lower: float32 [65536], P(('inst', 'row', 'col', 'sub')), parts along dimension 0, may hold values from -1 to 0
- span: float32 [65536], P(('inst', 'row', 'col', 'sub')), parts along dimension 0, may hold values from 0.5 to 4
- bound_kind: int32 [65536], P(('inst', 'row', 'col', 'sub')), parts along dimension 0, may hold values from 0 to 2
- demand: float32 [16, 16384], P(None, ('inst', 'row', 'col', 'sub')), parts along dimension 1, may hold values from -11 to 11
- restart_flags: int32 [8], replicated, may hold values from 0 to 1, as said below
Outputs:
- primal: float32 [16, 65536], P(None, ('inst', 'row', 'col', 'sub')), parts along dimension 1
- dual: float32 [16, 16384], P(None, ('inst', 'row', 'col', 'sub')), parts along dimension 1
The draws below stay inside these ranges and needn't reach their ends.
There are 2 independent parts, one for each index of `inst`. The reference program is written for one: setup_inputs(seed, part) draws one part's arguments, and reference() takes and returns one part's arrays. A program takes and returns all parts, laid end to end along the dimension named above; an argument that names none is the same for every part. Nothing has to cross between parts.
Inputs may be any that keep to these rules, and one draw needn't show every extreme that they name: Within each tile the 192 slots name distinct pairs of block_rows and block_cols. `block_count`: some tile of every part has exactly 192 live slots. `restart_flags`: some iteration in the first half of the 8 iterations restarts; the last iteration never does.
All inputs are finite; a program needn't handle non-finite values.
Results may differ from the reference program's by a relative error of at most 0.0007.
Values may be sent and summed in bfloat16 or wider, within the bound.
A program may use at most 64 MiB of HBM per device.

```python
import math
import jax
import jax.numpy as jnp
from jax import lax

BLK = 128
SCEN = 16
ITERS = 8
XB = 16
KMAX = 192
ROW_GROUPS = 2
COL_GROUPS = 8
GROUP_ROWS = 32
GROUP_COLS = 32
ROWS = 8192
COLS = 32768


def block_layout(key):
    base = jax.random.fold_in(key, 11)
    tile_keys = jax.random.split(base, ROW_GROUPS * COL_GROUPS)

    def one_tile(tile_key):
        return jax.random.permutation(tile_key, GROUP_ROWS * GROUP_COLS)[:KMAX]
    slots = jax.vmap(one_tile)(tile_keys)
    return slots.reshape(ROW_GROUPS, COL_GROUPS, KMAX).astype(jnp.int32)


def draw_block_rows(key, part):
    return (block_layout(key) // GROUP_COLS).astype(jnp.int32)


def draw_block_cols(key, part):
    return (block_layout(key) % GROUP_COLS).astype(jnp.int32)


def draw_block_count(key, part):
    first, second = jax.random.split(jax.random.fold_in(key, 5))
    shares = jax.random.randint(first, (ROW_GROUPS * COL_GROUPS,), 0, 8)
    counts = KMAX // (1 + shares)
    fullest = jax.random.randint(second, (), 0, ROW_GROUPS * COL_GROUPS)
    counts = jnp.where(jnp.arange(ROW_GROUPS * COL_GROUPS) == fullest, KMAX, counts)
    return counts.reshape(ROW_GROUPS, COL_GROUPS).astype(jnp.int32)


def draw_restart_flags(key, part):
    first, second = jax.random.split(jax.random.fold_in(key, 3))
    flags = jax.random.randint(first, (ITERS,), 0, 2)
    forced = jax.random.randint(second, (), 0, ITERS // 2)
    places = jnp.arange(ITERS)
    flags = jnp.where(places == forced, 1, flags)
    flags = jnp.where(places == ITERS - 1, 0, flags)
    return flags.astype(jnp.int32)


def draw_cost(key, part):
    key = jax.random.fold_in(key, 7)
    position = jnp.arange(COLS, dtype=jnp.float32) / (COLS - 1)
    values = jnp.clip(jax.random.normal(key, (COLS,), jnp.float32), -3.5, 3.5)
    ramp = 1.0 + 2.0 * position
    return values * ramp


def draw_demand(key, part):
    key = jax.random.fold_in(key, 9)
    position = jnp.arange(ROWS, dtype=jnp.float32)[None, :] / (ROWS - 1)
    values = jnp.clip(jax.random.normal(key, (SCEN, ROWS), jnp.float32), -3.5, 3.5)
    ramp = 1.0 + 2.0 * position
    return values * ramp


def with_ends(values, stream_key, least, high):
    shape = values.shape
    place = [jax.random.randint(jax.random.fold_in(stream_key, axis), (), 0, shape[axis]) for axis in range(len(shape))]
    values = values.at[tuple(place)].set(least)
    longest = shape.index(max(shape))
    place[longest] = (place[longest] + 1) % shape[longest]
    return values.at[tuple(place)].set(high)


def block_scale(own_key, dims, cuts, smallest, high):
    def one(dim, shards_of):
        heights = jax.random.uniform(jax.random.fold_in(jax.random.fold_in(own_key, 6), dim), (shards_of,), jnp.float32, smallest / len(cuts), high / len(cuts))
        return jnp.repeat(jnp.exp(heights), dims[dim] // shards_of).reshape((-1,) + (1,) * (len(dims) - dim - 1))

    loudness = one(*cuts[0])
    for cut in cuts[1:]:
        loudness = loudness * one(*cut)
    return loudness


def normal_values(rng, dims, deviation, most, cuts=(), kind=jnp.bfloat16):
    loudness = block_scale(rng, dims, cuts, -0.22, 0.18) if cuts else 1.0
    values = jax.random.normal(rng, dims, jnp.float32) * deviation * loudness
    return jnp.minimum(jnp.maximum(values, -most), most).astype(kind)


def setup_inputs(seed: int = 0, part: int = 0) -> dict:
    key_list = jax.random.split(jax.random.key(seed), 11)
    part_keys = jax.random.split(jax.random.fold_in(key_list[10], part), 11)
    a_blocks = normal_values(part_keys[0], (ROW_GROUPS, COL_GROUPS, KMAX, BLK, BLK), (2 * KMAX * BLK) ** -0.5, 0.02734375, ((0, 2), (1, 8)))
    block_rows = draw_block_rows(jax.random.fold_in(jax.random.fold_in(key_list[10], part), 71), part)
    block_cols = draw_block_cols(jax.random.fold_in(jax.random.fold_in(key_list[10], part), 71), part)
    block_count = draw_block_count(jax.random.fold_in(jax.random.fold_in(key_list[10], part), 71), part)
    cost = draw_cost(jax.random.fold_in(jax.random.fold_in(key_list[10], part), 71), part)
    lower = jnp.clip(-1.0 + 1.0 * jax.random.uniform(part_keys[5], (COLS,), jnp.float32) ** block_scale(part_keys[5], (COLS,), ((0, 16),), -0.2, 0.2), -1.0, 0.0)
    span = jnp.clip(jnp.exp(math.log(4.0) - 2.0794415 * jax.random.uniform(part_keys[6], (COLS,), jnp.float32) ** block_scale(part_keys[6], (COLS,), ((0, 16),), -0.2, 0.2)), 0.5, 4.0)
    bound_kind = with_ends(jax.random.randint(part_keys[7], (COLS,), 0, 3), jax.random.fold_in(part_keys[7], 1), 0, 2).astype(jnp.int32)
    demand = draw_demand(jax.random.fold_in(jax.random.fold_in(key_list[10], part), 71), part)
    restart_flags = draw_restart_flags(jax.random.fold_in(key_list[10], 71), part)
    return dict(a_blocks=a_blocks, block_rows=block_rows, block_cols=block_cols, block_count=block_count, cost=cost, lower=lower, span=span, bound_kind=bound_kind, demand=demand, restart_flags=restart_flags)


step_scale = 0.8
tiny = 1e-06

def clamp_box(values, low_side, high_side):
    return jnp.minimum(jnp.maximum(values, low_side), high_side)

def layout(block_rows, block_cols, block_count):
    tile_row = jnp.arange(ROW_GROUPS, dtype=jnp.int32)[:, None, None]
    tile_col = jnp.arange(COL_GROUPS, dtype=jnp.int32)[None, :, None]
    global_rows = tile_row * GROUP_ROWS + block_rows
    global_cols = (block_cols // XB * COL_GROUPS + tile_col) * XB + block_cols % XB
    live = jnp.arange(KMAX, dtype=jnp.int32)[None, None, :] < block_count[:, :, None]
    return (global_rows.astype(jnp.int32), global_cols.astype(jnp.int32), live)

def apply_forward(vector_half, a_blocks, block_rows, global_cols, live):
    pieces = lax.optimization_barrier(vector_half).astype(jnp.float32).reshape(SCEN, COLS // BLK, BLK)

    def one_group(inputs):
        blocks, rows_here, cols_here, live_here = inputs
        taken = jnp.take(pieces, cols_here.reshape(-1), axis=1)
        dense = blocks.reshape(-1, BLK, BLK).astype(jnp.float32)
        products = jnp.einsum('skb,kab->ksa', taken, dense, precision=lax.Precision.HIGHEST)
        products = products * live_here.reshape(-1)[:, None, None].astype(jnp.float32)
        return jax.ops.segment_sum(products, rows_here.reshape(-1), num_segments=GROUP_ROWS)
    stacked = lax.map(one_group, (a_blocks, block_rows, global_cols, live))
    stacked = stacked.reshape(ROWS // BLK, SCEN, BLK)
    return jnp.transpose(stacked, (1, 0, 2)).reshape(SCEN, ROWS)

def apply_adjoint(vector_half, a_blocks, global_rows, global_cols, live):
    pieces = lax.optimization_barrier(vector_half).astype(jnp.float32).reshape(SCEN, ROWS // BLK, BLK)

    def one_group(total, inputs):
        blocks, rows_here, cols_here, live_here = inputs
        taken = jnp.take(pieces, rows_here.reshape(-1), axis=1)
        dense = blocks.reshape(-1, BLK, BLK).astype(jnp.float32)
        products = jnp.einsum('ska,kab->ksb', taken, dense, precision=lax.Precision.HIGHEST)
        products = products * live_here.reshape(-1)[:, None, None].astype(jnp.float32)
        return (total + jax.ops.segment_sum(products, cols_here.reshape(-1), num_segments=COLS // BLK), None)
    start = jnp.zeros((COLS // BLK, SCEN, BLK), jnp.float32)
    total, unused = lax.scan(one_group, start, (a_blocks, global_rows, global_cols, live))
    return jnp.transpose(total, (1, 0, 2)).reshape(SCEN, COLS)

def reference(a_blocks, block_rows, block_cols, block_count, cost, lower, span, bound_kind, demand, restart_flags):
    global_rows, global_cols, live = layout(block_rows, block_cols, block_count)
    low_side = jnp.where(bound_kind == 2, -1e+30, lower)[None, :]
    high_side = jnp.where(bound_kind == 1, lower + span, 1e+30)[None, :]
    primal = jnp.zeros((SCEN, COLS), jnp.float32)
    dual = jnp.zeros((SCEN, ROWS), jnp.float32)
    primal_anchor = primal
    dual_anchor = dual
    primal_total = primal
    dual_total = dual
    count = jnp.zeros((), jnp.float32)
    weight = jnp.ones((SCEN, 1), jnp.float32)
    for step in range(ITERS):
        dual_half = dual.astype(jnp.bfloat16)
        gradient = apply_adjoint(dual_half, a_blocks, global_rows, global_cols, live)
        primal_new = clamp_box(primal - step_scale / weight * (cost[None, :] - gradient), low_side, high_side)
        primal_bar = (2.0 * primal_new - primal).astype(jnp.bfloat16)
        image = apply_forward(primal_bar, a_blocks, block_rows, global_cols, live)
        dual_new = jnp.maximum(dual + step_scale * weight * (demand - image), 0.0)
        primal_total = primal_total + primal_new
        dual_total = dual_total + dual_new
        count = count + 1.0
        primal_mean = primal_total / count
        dual_mean = dual_total / count
        primal_gap = primal_mean - primal_anchor
        dual_gap = dual_mean - dual_anchor
        gap_primal = lax.optimization_barrier(jnp.sum(primal_gap * primal_gap, axis=1))
        gap_dual = lax.optimization_barrier(jnp.sum(dual_gap * dual_gap, axis=1))
        ratio = jnp.sqrt((gap_dual / ROWS + tiny) / (gap_primal / COLS + tiny))
        restart = restart_flags[step] == 1
        weight = jnp.where(restart, jnp.sqrt(weight * ratio[:, None]), weight)
        primal = jnp.where(restart, primal_mean, primal_new)
        dual = jnp.where(restart, dual_mean, dual_new)
        primal_anchor = jnp.where(restart, primal_mean, primal_anchor)
        dual_anchor = jnp.where(restart, dual_mean, dual_anchor)
        primal_total = jnp.where(restart, 0.0, primal_total)
        dual_total = jnp.where(restart, 0.0, dual_total)
        count = jnp.where(restart, 0.0, count)
    return (primal, dual)
```

```python
import functools

import jax
import jax.numpy as jnp
from jax import lax
from jax.experimental import pallas as pl
from jax.experimental.pallas import tpu as pltpu
from jax.sharding import PartitionSpec as P

step_scale = 0.8
tiny = 1e-06
MESH = pl.DeviceIdType.MESH
BF = jnp.bfloat16
F32 = jnp.float32


def order_slots(key, source, live, groups, dead_source):
    slots = key.shape[0]
    places = jnp.arange(slots, dtype=jnp.int32)
    key = jnp.where(live, key, groups)
    source = jnp.where(live, source, dead_source)
    ahead = (key[None, :] < key[:, None]) | (
        (key[None, :] == key[:, None]) & (places[None, :] < places[:, None])
    )
    rank = jnp.sum(ahead.astype(jnp.int32), axis=1)
    hit = rank[None, :] == places[:, None]
    slot = jnp.sum(jnp.where(hit, places[None, :], 0), axis=1)
    sorted_key = jnp.sum(jnp.where(hit, key[None, :], 0), axis=1)
    sorted_source = jnp.sum(jnp.where(hit, source[None, :], 0), axis=1)
    before = jnp.concatenate([jnp.full((1,), -1, jnp.int32), sorted_key[:-1]])
    same = (before == sorted_key).astype(F32)
    names = jnp.arange(groups, dtype=jnp.int32)
    upto = jnp.sum((key[None, :] <= names[:, None]).astype(jnp.int32), axis=1)
    own = jnp.sum((key[None, :] == names[:, None]).astype(jnp.int32), axis=1)
    last = jnp.where(own > 0, upto - 1, slots)
    return slot, sorted_source, same, last


def kernel(
    sizes,
    index_ref,
    same_ref,
    last_row_ref,
    last_col_ref,
    flags_ref,
    blocks_hbm,
    cost_ref,
    lower_ref,
    span_ref,
    kind_ref,
    demand_ref,
    primal_out,
    dual_out,
    blocks,
    sums,
    bar,
    dual_all,
    bounds,
    primal,
    primal_new,
    primal_anchor,
    primal_total,
    dual,
    dual_anchor,
    dual_total,
    image_send,
    image_recv,
    adjoint_send,
    adjoint_recv,
    gap_all,
    gap_rows,
    weight_ref,
    copy_sem,
    bound_sems,
    dual_sems,
    gap_sems,
    image_sems,
    adjoint_sems,
    gap_row_sems,
):
    rows, cols, subs, iters, slots, own_rb, own_cb, unroll = sizes
    peers = cols * subs
    row_blocks = own_rb * peers
    col_blocks = own_cb * rows
    total_rows = own_rb * 128 * rows * peers
    total_cols = own_cb * 128 * rows * peers
    r = lax.axis_index("row")
    c = lax.axis_index("col") * subs + lax.axis_index("sub")

    load = pltpu.make_async_copy(blocks_hbm, blocks, copy_sem)
    load.start()

    def line(o):
        p = lax.rem(c + o, peers)
        return p, {"col": p // subs, "sub": lax.rem(p, subs)}

    def across(o):
        p = lax.rem(r + o, rows)
        return p, {"row": p}

    barrier = pltpu.get_barrier_semaphore()
    for o in range(1, peers):
        pl.semaphore_signal(barrier, inc=1, device_id=line(o)[1], device_id_type=MESH)
    for o in range(1, rows):
        pl.semaphore_signal(barrier, inc=1, device_id=across(o)[1], device_id_type=MESH)
    pl.semaphore_wait(barrier, peers + rows - 2)

    def push(src, dst, sems, mine, other, device):
        return pltpu.make_async_remote_copy(
            src_ref=src,
            dst_ref=dst,
            send_sem=sems.at[0, other],
            recv_sem=sems.at[1, mine],
            device_id=device,
            device_id_type=MESH,
        )

    kind = kind_ref[...]
    bounds[r, 0] = cost_ref[...]
    bounds[r, 1] = jnp.where(kind == 2, -1e30, lower_ref[...])
    bounds[r, 2] = jnp.where(kind == 1, lower_ref[...] + span_ref[...], 1e30)

    def bound_copy(o, dst):
        p, device = across(o)
        return push(bounds.at[r], bounds.at[dst(p)], bound_sems, dst(p), p, device)

    for o in range(1, rows):
        bound_copy(o, lambda p: r).start()
    zero = jnp.zeros((16, 128), F32)
    sums[slots] = zero
    bar[col_blocks] = zero.astype(BF)
    dual_all[row_blocks] = zero.astype(BF)
    weight_ref[...] = jnp.ones((16, 128), F32)
    dual[...] = jnp.zeros_like(dual)
    dual_anchor[...] = jnp.zeros_like(dual)
    dual_total[...] = jnp.zeros_like(dual)
    for o in range(1, rows):
        bound_copy(o, lambda p: p).wait_recv()
    for o in range(1, rows):
        bound_copy(o, lambda p: r).wait_send()

    for q in range(rows):
        for i in range(own_cb):
            j = q * own_cb + i
            new = -step_scale * bounds[q, 0, i : i + 1, :]
            new = jnp.minimum(
                jnp.maximum(new, bounds[q, 1, i : i + 1, :]), bounds[q, 2, i : i + 1, :]
            )
            new = jnp.broadcast_to(new, (16, 128))
            primal_new[j] = new
            bar[j] = (2.0 * new).astype(BF)
            primal[j] = zero
            primal_anchor[j] = zero
            primal_total[j] = zero
    load.wait()

    def product(source, which, contract):
        def body(i, acc):
            for u in range(unroll):
                k = i * unroll + u
                part = lax.dot_general(
                    source[index_ref[2 * which + 1, k]],
                    blocks[index_ref[2 * which, k]],
                    (((1,), (contract,)), ((), ())),
                    preferred_element_type=F32,
                )
                acc = acc * same_ref[which, k] + part
                sums[k] = acc
            return acc

        lax.fori_loop(0, slots // unroll, body, zero)

    def iteration(t, count):
        restart = flags_ref[t] == 1
        count = count + 1.0
        share = 1.0 / jnp.full((16, 128), count, F32)

        product(bar, 0, 1)

        def image_copy(o, dst):
            p, device = line(o)
            return push(
                image_send.at[p], image_recv.at[dst(p)], image_sems, dst(p), p, device
            )

        for o in range(1, peers):
            p, device = line(o)
            for i in range(own_rb):
                image_send[p, i] = sums[last_row_ref[p * own_rb + i]].astype(BF)
            image_copy(o, lambda p: c).start()

        def settle(j, gap):
            new = primal_new[j]
            total = primal_total[j] + new
            mean = total * share
            anchor = primal_anchor[j]
            primal[j] = jnp.where(restart, mean, new)
            primal_anchor[j] = jnp.where(restart, mean, anchor)
            primal_total[j] = jnp.where(restart, 0.0, total)
            away = mean - anchor
            return gap + away * away

        def settle_group(q, unused):
            def four(i, gap):
                for u in range(4):
                    gap = settle(q * own_cb + i * 4 + u, gap)
                return gap

            return lax.fori_loop(0, own_cb // 4, four, zero)

        gap_x = zero
        for o in range(1, rows):
            settle_group(lax.rem(r + o, rows), None)
        gap_x = settle_group(r, None)

        image = [sums[last_row_ref[c * own_rb + i]] for i in range(own_rb)]
        for o in range(1, peers):
            image_copy(o, lambda p: p).wait_recv()
        for o in range(1, peers):
            p, _ = line(o)
            for i in range(own_rb):
                image[i] = image[i] + image_recv[p, i].astype(F32)
        gap_y = zero
        weight = weight_ref[...]
        for i in range(own_rb):
            demand = demand_ref[:, i * 128 : (i + 1) * 128]
            new = jnp.maximum(dual[i] + step_scale * weight * (demand - image[i]), 0.0)
            total = dual_total[i] + new
            mean = total * share
            anchor = dual_anchor[i]
            value = jnp.where(restart, mean, new)
            dual[i] = value
            dual_all[c * own_rb + i] = value.astype(BF)
            dual_anchor[i] = jnp.where(restart, mean, anchor)
            dual_total[i] = jnp.where(restart, 0.0, total)
            away = mean - anchor
            gap_y = gap_y + away * away
        for o in range(1, peers):
            image_copy(o, lambda p: c).wait_send()

        @pl.when(t < iters - 1)
        def _():
            def dual_copy(o, dst):
                p, device = line(o)
                s = dst(p)
                return push(
                    dual_all.at[pl.ds(c * own_rb, own_rb)],
                    dual_all.at[pl.ds(s * own_rb, own_rb)],
                    dual_sems,
                    s,
                    p,
                    device,
                )

            for o in range(1, peers):
                dual_copy(o, lambda p: c).start()

            low = lax.broadcasted_iota(jnp.int32, (16, 128), 1) < 64
            gap_all[c] = jnp.where(
                low,
                gap_x + pltpu.roll(gap_x, 64, 1),
                gap_y + pltpu.roll(gap_y, 64, 1),
            )

            def gap_copy(o, dst):
                p, device = line(o)
                s = dst(p)
                return push(gap_all.at[c], gap_all.at[s], gap_sems, s, p, device)

            for o in range(1, peers):
                gap_copy(o, lambda p: c).start()
            for o in range(1, peers):
                dual_copy(o, lambda p: p).wait_recv()

            product(dual_all, 1, 0)

            slot = lax.rem(t, 2)
            def adjoint_copy(o, dst):
                p, device = across(o)
                s = dst(p)
                return push(
                    adjoint_send,
                    adjoint_recv.at[slot, s],
                    adjoint_sems.at[slot],
                    s,
                    p,
                    device,
                )

            def pack(i, unused):
                for u in range(8):
                    j = i * 8 + u
                    adjoint_send[j] = sums[last_col_ref[j]].astype(BF)
                return unused

            lax.fori_loop(0, col_blocks // 8, pack, 0)
            for o in range(1, rows):
                adjoint_copy(o, lambda p: r).start()

            for o in range(1, peers):
                gap_copy(o, lambda p: p).wait_recv()
            gap = gap_all[0]
            for p in range(1, peers):
                gap = gap + gap_all[p]
            gap_rows[slot, r] = gap

            def gap_row_copy(o, dst):
                p, device = across(o)
                s = dst(p)
                return push(
                    gap_rows.at[slot, r],
                    gap_rows.at[slot, s],
                    gap_row_sems.at[slot],
                    s,
                    p,
                    device,
                )

            for o in range(1, rows):
                gap_row_copy(o, lambda p: r).start()
            for o in range(1, rows):
                gap_row_copy(o, lambda p: p).wait_recv()
            gap = gap_rows[slot, 0]
            for p in range(1, rows):
                gap = gap + gap_rows[slot, p]
            sum_x = jnp.sum(jnp.where(low, gap, 0.0), axis=1, keepdims=True)
            sum_y = jnp.sum(jnp.where(low, 0.0, gap), axis=1, keepdims=True)
            sum_x = jnp.broadcast_to(sum_x, (16, 128))
            sum_y = jnp.broadcast_to(sum_y, (16, 128))
            ratio = jnp.sqrt((sum_y / total_rows + tiny) / (sum_x / total_cols + tiny))
            fresh = jnp.where(restart, jnp.sqrt(weight * ratio), weight)
            weight_ref[...] = fresh
            stride = step_scale / fresh

            for o in range(1, rows):
                adjoint_copy(o, lambda p: p).wait_recv()

            for q in range(rows):

                def update(i, unused):
                    for u in range(4):
                        n = i * 4 + u
                        j = q * own_cb + n
                        gradient = sums[last_col_ref[j]]
                        for o in range(1, rows):
                            p, _ = across(o)
                            gradient = gradient + adjoint_recv[slot, p, j].astype(F32)
                        old = primal[j]
                        new = old - stride * (bounds[q, 0, pl.ds(n, 1), :] - gradient)
                        new = jnp.maximum(new, bounds[q, 1, pl.ds(n, 1), :])
                        new = jnp.minimum(new, bounds[q, 2, pl.ds(n, 1), :])
                        primal_new[j] = new
                        bar[j] = (2.0 * new - old).astype(BF)
                    return unused

                lax.fori_loop(0, own_cb // 4, update, 0)

            for o in range(1, peers):
                dual_copy(o, lambda p: c).wait_send()
                gap_copy(o, lambda p: c).wait_send()
            for o in range(1, rows):
                adjoint_copy(o, lambda p: r).wait_send()
                gap_row_copy(o, lambda p: r).wait_send()

        return jnp.where(restart, 0.0, count)

    lax.fori_loop(0, iters, iteration, jnp.zeros((), F32))
    for i in range(own_cb):
        primal_out[:, i * 128 : (i + 1) * 128] = primal[r * own_cb + i]
    for i in range(own_rb):
        dual_out[:, i * 128 : (i + 1) * 128] = dual[i]


def shards(
    rows,
    cols,
    subs,
    a_blocks,
    block_rows,
    block_cols,
    block_count,
    cost,
    lower,
    span,
    bound_kind,
    demand,
    restart_flags,
):
    blocks = a_blocks[0, 0]
    slots = blocks.shape[0]
    peers = cols * subs
    own_rb = demand.shape[1] // 128
    own_cb = cost.shape[0] // 128
    row_blocks = own_rb * peers
    col_blocks = own_cb * rows
    iters = restart_flags.shape[0]
    unroll = 32 if slots % 32 == 0 else 1
    live = jnp.arange(slots) < block_count[0, 0]
    row_list = block_rows[0, 0]
    col_list = block_cols[0, 0]
    slot_f, source_f, same_f, last_row = order_slots(
        row_list, col_list, live, row_blocks, col_blocks
    )
    slot_a, source_a, same_a, last_col = order_slots(
        col_list, row_list, live, col_blocks, row_blocks
    )
    index = jnp.stack([slot_f, source_f, slot_a, source_a])
    same = jnp.stack([same_f, same_a])
    sizes = (rows, cols, subs, iters, slots, own_rb, own_cb, unroll)
    smem = pl.BlockSpec(memory_space=pltpu.SMEM)
    vmem = pl.BlockSpec(memory_space=pltpu.VMEM)
    dma = pltpu.SemaphoreType.DMA
    tile = (16, 128)
    call = pl.pallas_call(
        functools.partial(kernel, sizes),
        out_shape=(
            jax.ShapeDtypeStruct((16, own_cb * 128), F32),
            jax.ShapeDtypeStruct((16, own_rb * 128), F32),
        ),
        in_specs=[smem] * 5 + [pl.BlockSpec(memory_space=pl.ANY)] + [vmem] * 5,
        out_specs=(vmem, vmem),
        scratch_shapes=[
            pltpu.VMEM((slots, 128, 128), BF),
            pltpu.VMEM((slots + 1,) + tile, F32),
            pltpu.VMEM((col_blocks + 1,) + tile, BF),
            pltpu.VMEM((row_blocks + 1,) + tile, BF),
            pltpu.VMEM((rows, 3, own_cb, 128), F32),
            pltpu.VMEM((col_blocks,) + tile, F32),
            pltpu.VMEM((col_blocks,) + tile, F32),
            pltpu.VMEM((col_blocks,) + tile, F32),
            pltpu.VMEM((col_blocks,) + tile, F32),
            pltpu.VMEM((own_rb,) + tile, F32),
            pltpu.VMEM((own_rb,) + tile, F32),
            pltpu.VMEM((own_rb,) + tile, F32),
            pltpu.VMEM((peers, own_rb) + tile, BF),
            pltpu.VMEM((peers, own_rb) + tile, BF),
            pltpu.VMEM((col_blocks,) + tile, BF),
            pltpu.VMEM((2, rows, col_blocks) + tile, BF),
            pltpu.VMEM((peers,) + tile, F32),
            pltpu.VMEM((2, rows) + tile, F32),
            pltpu.VMEM(tile, F32),
            dma,
            dma((2, rows)),
            dma((2, peers)),
            dma((2, peers)),
            dma((2, peers)),
            dma((2, 2, rows)),
            dma((2, 2, rows)),
        ],
        compiler_params=pltpu.CompilerParams(
            collective_id=0,
            has_side_effects=True,
            vmem_limit_bytes=40 * 1024 * 1024,
        ),
    )
    as_blocks = lambda v: v.reshape(own_cb, 128)
    return call(
        index,
        same,
        last_row,
        last_col,
        restart_flags,
        blocks,
        as_blocks(cost),
        as_blocks(lower),
        as_blocks(span),
        as_blocks(bound_kind),
        demand,
    )


def solution(mesh):
    placed = (
        P(("inst", "row"), ("col", "sub"), None, None, None),
        P(("inst", "row"), ("col", "sub"), None),
        P(("inst", "row"), ("col", "sub"), None),
        P(("inst", "row"), ("col", "sub")),
        P(("inst", "row", "col", "sub")),
        P(("inst", "row", "col", "sub")),
        P(("inst", "row", "col", "sub")),
        P(("inst", "row", "col", "sub")),
        P(None, ("inst", "row", "col", "sub")),
        P(),
    )
    shape = mesh.shape
    return jax.shard_map(
        functools.partial(shards, shape["row"], shape["col"], shape["sub"]),
        mesh=mesh,
        in_specs=placed,
        out_specs=(P(None, ("inst", "row", "col", "sub")), P(None, ("inst", "row", "col", "sub"))),
        check_vma=False,
    )
```

```python
import functools

import jax
import jax.numpy as jnp
from jax import lax
from jax.experimental import pallas as pl
from jax.experimental.pallas import tpu as pltpu
from jax.sharding import PartitionSpec as P

step_scale = 0.8
tiny = 1e-06
MESH = pl.DeviceIdType.MESH
BF = jnp.bfloat16
F32 = jnp.float32


def order_slots(key, source, live, groups, dead_source):
    slots = key.shape[0]
    places = jnp.arange(slots, dtype=jnp.int32)
    key = jnp.where(live, key, groups)
    source = jnp.where(live, source, dead_source)
    ahead = (key[None, :] < key[:, None]) | (
        (key[None, :] == key[:, None]) & (places[None, :] < places[:, None])
    )
    rank = jnp.sum(ahead.astype(jnp.int32), axis=1)
    hit = rank[None, :] == places[:, None]
    slot = jnp.sum(jnp.where(hit, places[None, :], 0), axis=1)
    sorted_key = jnp.sum(jnp.where(hit, key[None, :], 0), axis=1)
    sorted_source = jnp.sum(jnp.where(hit, source[None, :], 0), axis=1)
    before = jnp.concatenate([jnp.full((1,), -1, jnp.int32), sorted_key[:-1]])
    same = (before == sorted_key).astype(F32)
    names = jnp.arange(groups, dtype=jnp.int32)
    upto = jnp.sum((key[None, :] <= names[:, None]).astype(jnp.int32), axis=1)
    own = jnp.sum((key[None, :] == names[:, None]).astype(jnp.int32), axis=1)
    last = jnp.where(own > 0, upto - 1, slots)
    return slot, sorted_source, same, last


def kernel(
    sizes,
    index_ref,
    same_ref,
    last_row_ref,
    last_col_ref,
    flags_ref,
    blocks_hbm,
    cost_hbm,
    lower_hbm,
    span_hbm,
    kind_hbm,
    demand_hbm,
    primal_out,
    dual_out,
    blocks,
    flipped,
    vectors,
    kind_ref,
    demand_ref,
    sums,
    bar,
    dual_all,
    bounds,
    primal,
    primal_new,
    primal_anchor,
    primal_total,
    dual,
    dual_anchor,
    dual_total,
    pair_send,
    pair_recv,
    image_send,
    image_recv,
    adjoint_send,
    adjoint_recv,
    gap_line,
    gap_group,
    weight_ref,
    copy_sems,
    bound_sems,
    pair_sems,
    image_sems,
    dual_sems,
    forward_sems,
    gap_sems,
    group_sems,
    adjoint_sems,
):
    rows, cols, subs, iters, slots, own_rb, own_cb, unroll, chunk = sizes
    group = rows * subs
    row_blocks = own_rb * cols * subs
    col_blocks = own_cb * rows
    chunks = col_blocks // chunk
    total_rows = own_rb * 128 * rows * cols * subs
    total_cols = own_cb * 128 * rows * cols * subs
    r = lax.axis_index("row")
    z = lax.axis_index("col")
    s = lax.axis_index("sub")
    g = r * subs + s

    loads = [
        pltpu.make_async_copy(cost_hbm, vectors.at[0], copy_sems.at[0]),
        pltpu.make_async_copy(lower_hbm, vectors.at[1], copy_sems.at[1]),
        pltpu.make_async_copy(span_hbm, vectors.at[2], copy_sems.at[2]),
        pltpu.make_async_copy(kind_hbm, kind_ref, copy_sems.at[3]),
        pltpu.make_async_copy(demand_hbm, demand_ref, copy_sems.at[4]),
        pltpu.make_async_copy(blocks_hbm, blocks, copy_sems.at[5]),
    ]
    for load in loads:
        load.start()

    def along(o):
        if cols & (cols - 1):
            return lax.rem(z + o, cols)
        p = z
        bit = 1
        while bit < cols:
            if o & bit:
                p = p + bit * (1 - 2 * lax.rem(lax.div(z, bit), 2))
            bit *= 2
        return p

    def across(o):
        return lax.rem(r + o, rows)

    def beside(o):
        return lax.rem(s + o, subs)

    def around(o):
        p = lax.rem(g + o, group)
        return p, {"row": lax.div(p, subs), "sub": lax.rem(p, subs)}

    barrier = pltpu.get_barrier_semaphore()
    for o in range(1, cols):
        pl.semaphore_signal(barrier, inc=1, device_id={"col": along(o)}, device_id_type=MESH)
    for o in range(1, group):
        pl.semaphore_signal(barrier, inc=1, device_id=around(o)[1], device_id_type=MESH)
    pl.semaphore_wait(barrier, cols + group - 2)

    def push(src, dst, send_sem, recv_sem, device):
        return pltpu.make_async_remote_copy(
            src_ref=src,
            dst_ref=dst,
            send_sem=send_sem,
            recv_sem=recv_sem,
            device_id=device,
            device_id_type=MESH,
        )

    def bound_copy(o, mine):
        p = across(o)
        n = r if mine else p
        return push(
            bounds.at[r], bounds.at[n], bound_sems.at[0, p], bound_sems.at[1, n], {"row": p}
        )

    def pair_copy(o, q, mine):
        p = beside(o)
        n = s if mine else p
        return push(
            pair_send.at[p, q],
            pair_recv.at[n, q],
            pair_sems.at[0, p, q],
            pair_sems.at[1, n, q],
            {"sub": p},
        )

    def image_copy(o, mine):
        p = along(o)
        n = z if mine else p
        return push(
            image_send.at[p],
            image_recv.at[n],
            image_sems.at[0, p],
            image_sems.at[1, n],
            {"col": p},
        )

    def dual_part(q, n):
        return dual_all.at[pl.ds((q * subs + n) * own_rb, own_rb)]

    def dual_copy(o, mine):
        p = along(o)
        n = z if mine else p
        return push(
            dual_part(z, s), dual_part(n, s), dual_sems.at[0, p], dual_sems.at[1, n], {"col": p}
        )

    def forward_copy(o, q, mine):
        p = beside(o)
        n = s if mine else p
        return push(
            dual_part(q, s),
            dual_part(q, n),
            forward_sems.at[0, p, q],
            forward_sems.at[1, n, q],
            {"sub": p},
        )

    def gap_copy(o, mine):
        p = along(o)
        n = z if mine else p
        return push(
            gap_line.at[z], gap_line.at[n], gap_sems.at[0, p], gap_sems.at[1, n], {"col": p}
        )

    def group_copy(o, slot, mine):
        p, device = around(o)
        n = g if mine else p
        return push(
            gap_group.at[slot, g],
            gap_group.at[slot, n],
            group_sems.at[slot, 0, p],
            group_sems.at[slot, 1, n],
            device,
        )

    def adjoint_copy(o, slot, part, mine):
        p = across(o)
        n = r if mine else p
        span = pl.ds(part * chunk, chunk)
        return push(
            adjoint_send.at[span],
            adjoint_recv.at[slot, n, span],
            adjoint_sems.at[slot, 0, p, part],
            adjoint_sems.at[slot, 1, n, part],
            {"row": p},
        )

    for load in loads[:4]:
        load.wait()
    kind = kind_ref[...]
    bounds[r, 0] = vectors[0]
    bounds[r, 1] = jnp.where(kind == 2, -1e30, vectors[1])
    bounds[r, 2] = jnp.where(kind == 1, vectors[1] + vectors[2], 1e30)
    for o in range(1, rows):
        bound_copy(o, True).start()
    zero = jnp.zeros((16, 128), F32)
    none = jnp.zeros((16, 128), BF)
    sums[slots] = zero
    bar[col_blocks] = none
    dual_all[row_blocks] = none
    weight_ref[...] = jnp.ones((16, 128), F32)
    dual[...] = jnp.zeros_like(dual)
    dual_anchor[...] = jnp.zeros_like(dual)
    dual_total[...] = jnp.zeros_like(dual)
    loads[4].wait()
    loads[5].wait()

    def flip(i, unused):
        for u in range(16):
            k = i * 16 + u
            flipped[k] = blocks[index_ref[0, k]].T
        return unused

    lax.fori_loop(0, slots // 16, flip, 0)

    for o in range(1, rows):
        bound_copy(o, False).wait_recv()
    for o in range(1, rows):
        bound_copy(o, True).wait_send()

    for q in range(rows):
        for i in range(own_cb):
            j = q * own_cb + i
            new = -step_scale * bounds[q, 0, i : i + 1, :]
            new = jnp.minimum(
                jnp.maximum(new, bounds[q, 1, i : i + 1, :]), bounds[q, 2, i : i + 1, :]
            )
            new = jnp.broadcast_to(new, (16, 128))
            primal_new[j] = new
            bar[j] = (2.0 * new).astype(BF)
            primal[j] = zero
            primal_anchor[j] = zero
            primal_total[j] = zero

    def product(source, which, pair_of):
        def body(i, acc):
            for u in range(0, unroll, 2):
                k = i * unroll + u
                first = source[index_ref[2 * which + 1, k]]
                second = source[index_ref[2 * which + 1, k + 1]]
                left = jnp.concatenate(
                    [
                        jnp.concatenate([first, none], 1),
                        jnp.concatenate([none, second], 1),
                    ],
                    0,
                )
                parts = jnp.dot(left, pair_of(k), preferred_element_type=F32)
                acc = acc * same_ref[which, k] + parts[:16]
                sums[k] = acc
                acc = acc * same_ref[which, k + 1] + parts[16:]
                sums[k + 1] = acc
            return acc

        lax.fori_loop(0, slots // unroll, body, zero)

    def forward_pair(k):
        return jnp.concatenate([flipped[k], flipped[k + 1]], 0)

    def adjoint_pair(k):
        return jnp.concatenate([blocks[index_ref[2, k]], blocks[index_ref[2, k + 1]]], 0)

    def iteration(t, count):
        restart = flags_ref[t] == 1
        slot = lax.rem(t, 2)
        count = count + 1.0
        share = 1.0 / jnp.full((16, 128), count, F32)

        product(bar, 0, forward_pair)
        order = [along(o) for o in range(cols - 1, 0, -1)] + [z]
        for q in order:
            for o in range(1, subs):
                p = beside(o)
                for i in range(own_rb):
                    pair_send[p, q, i] = sums[last_row_ref[(q * subs + p) * own_rb + i]]
                pair_copy(o, q, True).start()

        def pair_sum(q):
            for o in range(1, subs):
                pair_copy(o, q, False).wait_recv()
            total = []
            for i in range(own_rb):
                value = sums[last_row_ref[(q * subs + s) * own_rb + i]]
                for o in range(1, subs):
                    value = value + pair_recv[beside(o), q, i]
                total.append(value)
            return total

        for o in range(cols - 1, 0, -1):
            q = along(o)
            total = pair_sum(q)
            for i in range(own_rb):
                image_send[q, i] = total[i].astype(BF)
            image_copy(o, True).start()
        image = pair_sum(z)

        def settle(j, gap):
            new = primal_new[j]
            total = primal_total[j] + new
            mean = total * share
            anchor = primal_anchor[j]
            primal[j] = jnp.where(restart, mean, new)
            primal_anchor[j] = jnp.where(restart, mean, anchor)
            primal_total[j] = jnp.where(restart, 0.0, total)
            away = mean - anchor
            return gap + away * away

        def settle_group(q):
            def four(i, gap):
                for u in range(4):
                    gap = settle(q * own_cb + i * 4 + u, gap)
                return gap

            return lax.fori_loop(0, own_cb // 4, four, zero)

        for o in range(1, rows):
            settle_group(across(o))
        gap_x = settle_group(r)

        for o in range(1, cols):
            image_copy(o, False).wait_recv()
            for i in range(own_rb):
                image[i] = image[i] + image_recv[along(o), i].astype(F32)
        gap_y = zero
        weight = weight_ref[...]
        for i in range(own_rb):
            demand = demand_ref[:, i * 128 : (i + 1) * 128]
            new = jnp.maximum(dual[i] + step_scale * weight * (demand - image[i]), 0.0)
            total = dual_total[i] + new
            mean = total * share
            anchor = dual_anchor[i]
            value = jnp.where(restart, mean, new)
            dual[i] = value
            dual_all[(z * subs + s) * own_rb + i] = value.astype(BF)
            dual_anchor[i] = jnp.where(restart, mean, anchor)
            dual_total[i] = jnp.where(restart, 0.0, total)
            away = mean - anchor
            gap_y = gap_y + away * away

        @pl.when(t < iters - 1)
        def _():
            for o in range(cols - 1, 0, -1):
                dual_copy(o, True).start()
            for o in range(1, subs):
                forward_copy(o, z, True).start()

            low = lax.broadcasted_iota(jnp.int32, (16, 128), 1) < 64
            gap_line[z] = jnp.where(
                low,
                gap_x + pltpu.roll(gap_x, 64, 1),
                gap_y + pltpu.roll(gap_y, 64, 1),
            )
            for o in range(cols - 1, 0, -1):
                gap_copy(o, True).start()

            for o in range(1, cols):
                dual_copy(o, False).wait_recv()
                for n in range(1, subs):
                    forward_copy(n, along(o), True).start()
            for o in range(cols):
                for n in range(1, subs):
                    forward_copy(n, along(o), False).wait_recv()

            product(dual_all, 1, adjoint_pair)

            for o in range(1, cols):
                gap_copy(o, False).wait_recv()
            gap = gap_line[0]
            for p in range(1, cols):
                gap = gap + gap_line[p]
            gap_group[slot, g] = gap
            for o in range(1, group):
                group_copy(o, slot, True).start()

            for part in range(chunks):
                for u in range(chunk):
                    j = part * chunk + u
                    adjoint_send[j] = sums[last_col_ref[j]].astype(BF)
                for o in range(1, rows):
                    adjoint_copy(o, slot, part, True).start()

            for o in range(1, group):
                group_copy(o, slot, False).wait_recv()
            gap = gap_group[slot, 0]
            for p in range(1, group):
                gap = gap + gap_group[slot, p]
            sum_x = jnp.sum(jnp.where(low, gap, 0.0), axis=1, keepdims=True)
            sum_y = jnp.sum(jnp.where(low, 0.0, gap), axis=1, keepdims=True)
            sum_x = jnp.broadcast_to(sum_x, (16, 128))
            sum_y = jnp.broadcast_to(sum_y, (16, 128))
            ratio = jnp.sqrt((sum_y / total_rows + tiny) / (sum_x / total_cols + tiny))
            fresh = jnp.where(restart, jnp.sqrt(weight * ratio), weight)
            weight_ref[...] = fresh
            stride = step_scale / fresh

            for part in range(chunks):
                for o in range(1, rows):
                    adjoint_copy(o, slot, part, False).wait_recv()
                for u in range(chunk):
                    j = part * chunk + u
                    q, n = j // own_cb, j % own_cb
                    gradient = sums[last_col_ref[j]]
                    for o in range(1, rows):
                        gradient = gradient + adjoint_recv[slot, across(o), j].astype(F32)
                    old = primal[j]
                    new = old - stride * (bounds[q, 0, n : n + 1, :] - gradient)
                    new = jnp.maximum(new, bounds[q, 1, n : n + 1, :])
                    new = jnp.minimum(new, bounds[q, 2, n : n + 1, :])
                    primal_new[j] = new
                    bar[j] = (2.0 * new - old).astype(BF)

            for o in range(1, cols):
                dual_copy(o, True).wait_send()
                gap_copy(o, True).wait_send()
            for o in range(1, subs):
                for q in order:
                    forward_copy(o, q, True).wait_send()
            for o in range(1, group):
                group_copy(o, slot, True).wait_send()
            for o in range(1, rows):
                for part in range(chunks):
                    adjoint_copy(o, slot, part, True).wait_send()

        for o in range(1, cols):
            image_copy(o, True).wait_send()
        for o in range(1, subs):
            for q in order:
                pair_copy(o, q, True).wait_send()
        return jnp.where(restart, 0.0, count)

    lax.fori_loop(0, iters, iteration, jnp.zeros((), F32))
    for i in range(own_cb):
        primal_out[:, i * 128 : (i + 1) * 128] = primal[r * own_cb + i]
    for i in range(own_rb):
        dual_out[:, i * 128 : (i + 1) * 128] = dual[i]


def shards(
    rows,
    cols,
    subs,
    a_blocks,
    block_rows,
    block_cols,
    block_count,
    cost,
    lower,
    span,
    bound_kind,
    demand,
    restart_flags,
):
    blocks = a_blocks[0, 0]
    slots = blocks.shape[0]
    peers = cols * subs
    own_rb = demand.shape[1] // 128
    own_cb = cost.shape[0] // 128
    row_blocks = own_rb * peers
    col_blocks = own_cb * rows
    iters = restart_flags.shape[0]
    unroll = 96
    chunk = own_cb // 2
    live = jnp.arange(slots) < block_count[0, 0]
    row_list = block_rows[0, 0]
    col_list = block_cols[0, 0]
    slot_f, source_f, same_f, last_row = order_slots(
        row_list, col_list, live, row_blocks, col_blocks
    )
    slot_a, source_a, same_a, last_col = order_slots(
        col_list, row_list, live, col_blocks, row_blocks
    )
    index = jnp.stack([slot_f, source_f, slot_a, source_a])
    same = jnp.stack([same_f, same_a])
    sizes = (rows, cols, subs, iters, slots, own_rb, own_cb, unroll, chunk)
    smem = pl.BlockSpec(memory_space=pltpu.SMEM)
    vmem = pl.BlockSpec(memory_space=pltpu.VMEM)
    dma = pltpu.SemaphoreType.DMA
    tile = (16, 128)
    call = pl.pallas_call(
        functools.partial(kernel, sizes),
        out_shape=(
            jax.ShapeDtypeStruct((16, own_cb * 128), F32),
            jax.ShapeDtypeStruct((16, own_rb * 128), F32),
        ),
        in_specs=[smem] * 5 + [pl.BlockSpec(memory_space=pl.ANY)] * 6,
        out_specs=(vmem, vmem),
        scratch_shapes=[
            pltpu.VMEM((slots, 128, 128), BF),
            pltpu.VMEM((slots, 128, 128), BF),
            pltpu.VMEM((3, own_cb, 128), F32),
            pltpu.VMEM((own_cb, 128), jnp.int32),
            pltpu.VMEM((16, own_rb * 128), F32),
            pltpu.VMEM((slots + 1,) + tile, F32),
            pltpu.VMEM((col_blocks + 1,) + tile, BF),
            pltpu.VMEM((row_blocks + 1,) + tile, BF),
            pltpu.VMEM((rows, 3, own_cb, 128), F32),
            pltpu.VMEM((col_blocks,) + tile, F32),
            pltpu.VMEM((col_blocks,) + tile, F32),
            pltpu.VMEM((col_blocks,) + tile, F32),
            pltpu.VMEM((col_blocks,) + tile, F32),
            pltpu.VMEM((own_rb,) + tile, F32),
            pltpu.VMEM((own_rb,) + tile, F32),
            pltpu.VMEM((own_rb,) + tile, F32),
            pltpu.VMEM((subs, cols, own_rb) + tile, F32),
            pltpu.VMEM((subs, cols, own_rb) + tile, F32),
            pltpu.VMEM((cols, own_rb) + tile, BF),
            pltpu.VMEM((cols, own_rb) + tile, BF),
            pltpu.VMEM((col_blocks,) + tile, BF),
            pltpu.VMEM((2, rows, col_blocks) + tile, BF),
            pltpu.VMEM((cols,) + tile, F32),
            pltpu.VMEM((2, rows * subs) + tile, F32),
            pltpu.VMEM(tile, F32),
            dma((6,)),
            dma((2, rows)),
            dma((2, subs, cols)),
            dma((2, cols)),
            dma((2, cols)),
            dma((2, subs, cols)),
            dma((2, cols)),
            dma((2, 2, rows * subs)),
            dma((2, 2, rows, col_blocks // chunk)),
        ],
        compiler_params=pltpu.CompilerParams(
            collective_id=0,
            has_side_effects=True,
            vmem_limit_bytes=60 * 1024 * 1024,
        ),
    )
    as_blocks = lambda v: v.reshape(own_cb, 128)
    return call(
        index,
        same,
        last_row,
        last_col,
        restart_flags,
        blocks,
        as_blocks(cost),
        as_blocks(lower),
        as_blocks(span),
        as_blocks(bound_kind),
        demand,
    )


def solution(mesh):
    placed = (
        P(("inst", "row"), ("col", "sub"), None, None, None),
        P(("inst", "row"), ("col", "sub"), None),
        P(("inst", "row"), ("col", "sub"), None),
        P(("inst", "row"), ("col", "sub")),
        P(("inst", "row", "col", "sub")),
        P(("inst", "row", "col", "sub")),
        P(("inst", "row", "col", "sub")),
        P(("inst", "row", "col", "sub")),
        P(None, ("inst", "row", "col", "sub")),
        P(),
    )
    shape = mesh.shape
    return jax.shard_map(
        functools.partial(shards, shape["row"], shape["col"], shape["sub"]),
        mesh=mesh,
        in_specs=placed,
        out_specs=(P(None, ("inst", "row", "col", "sub")), P(None, ("inst", "row", "col", "sub"))),
        check_vma=False,
    )
```

```python
import functools

import jax
import jax.numpy as jnp
from jax import lax
from jax.experimental import pallas as pl
from jax.experimental.pallas import tpu as pltpu
from jax.sharding import PartitionSpec as P

step_scale = 0.8
tiny = 1e-06
MESH = pl.DeviceIdType.MESH
BF = jnp.bfloat16
F32 = jnp.float32


def order_slots(key, source, live, groups, dead_source):
    slots = key.shape[0]
    places = jnp.arange(slots, dtype=jnp.int32)
    key = jnp.where(live, key, groups)
    source = jnp.where(live, source, dead_source)
    ahead = (key[None, :] < key[:, None]) | (
        (key[None, :] == key[:, None]) & (places[None, :] < places[:, None])
    )
    rank = jnp.sum(ahead.astype(jnp.int32), axis=1)
    hit = rank[None, :] == places[:, None]
    slot = jnp.sum(jnp.where(hit, places[None, :], 0), axis=1)
    sorted_key = jnp.sum(jnp.where(hit, key[None, :], 0), axis=1)
    sorted_source = jnp.sum(jnp.where(hit, source[None, :], 0), axis=1)
    before = jnp.concatenate([jnp.full((1,), -1, jnp.int32), sorted_key[:-1]])
    same = (before == sorted_key).astype(F32)
    names = jnp.arange(groups, dtype=jnp.int32)
    upto = jnp.sum((key[None, :] <= names[:, None]).astype(jnp.int32), axis=1)
    own = jnp.sum((key[None, :] == names[:, None]).astype(jnp.int32), axis=1)
    last = jnp.where(own > 0, upto - 1, slots)
    return slot, sorted_source, same, last


def kernel(
    sizes,
    index_ref,
    same_ref,
    last_row_ref,
    last_col_ref,
    flags_ref,
    blocks_hbm,
    cost_hbm,
    lower_hbm,
    span_hbm,
    kind_hbm,
    demand_hbm,
    primal_out,
    dual_out,
    blocks,
    flipped,
    vectors,
    kind_ref,
    demand_ref,
    sums,
    bar,
    dual_all,
    bounds,
    primal,
    primal_new,
    primal_anchor,
    primal_total,
    dual,
    dual_anchor,
    dual_total,
    pair_send,
    pair_recv,
    image_send,
    image_recv,
    adjoint_send,
    adjoint_recv,
    gap_line,
    gap_group,
    weight_ref,
    copy_sems,
    bound_sems,
    pair_sems,
    image_sems,
    dual_sems,
    gap_sems,
    group_sems,
    adjoint_sems,
):
    rows, cols, subs, iters, slots, own_rb, own_cb, unroll, chunk = sizes
    group = rows * subs
    row_blocks = own_rb * cols * subs
    col_blocks = own_cb * rows
    chunks = col_blocks // chunk
    total_rows = own_rb * 128 * rows * cols * subs
    total_cols = own_cb * 128 * rows * cols * subs
    r = lax.axis_index("row")
    z = lax.axis_index("col")
    s = lax.axis_index("sub")
    g = r * subs + s

    loads = [
        pltpu.make_async_copy(cost_hbm, vectors.at[0], copy_sems.at[0]),
        pltpu.make_async_copy(lower_hbm, vectors.at[1], copy_sems.at[1]),
        pltpu.make_async_copy(span_hbm, vectors.at[2], copy_sems.at[2]),
        pltpu.make_async_copy(kind_hbm, kind_ref, copy_sems.at[3]),
        pltpu.make_async_copy(demand_hbm, demand_ref, copy_sems.at[4]),
        pltpu.make_async_copy(blocks_hbm, blocks, copy_sems.at[5]),
    ]
    for load in loads:
        load.start()

    def along(o):
        if cols & (cols - 1):
            return lax.rem(z + o, cols)
        p = z
        bit = 1
        while bit < cols:
            if o & bit:
                p = p + bit * (1 - 2 * lax.rem(lax.div(z, bit), 2))
            bit *= 2
        return p

    def across(o):
        return lax.rem(r + o, rows)

    def beside(o):
        return lax.rem(s + o, subs)

    def around(o):
        p = lax.rem(g + o, group)
        return p, {"row": lax.div(p, subs), "sub": lax.rem(p, subs)}

    barrier = pltpu.get_barrier_semaphore()
    for o in range(1, cols):
        pl.semaphore_signal(barrier, inc=1, device_id={"col": along(o)}, device_id_type=MESH)
    for o in range(1, group):
        pl.semaphore_signal(barrier, inc=1, device_id=around(o)[1], device_id_type=MESH)
    for o in range(1, cols):
        for n in range(1, subs):
            pl.semaphore_signal(
                barrier,
                inc=1,
                device_id={"col": along(o), "sub": beside(n)},
                device_id_type=MESH,
            )
    pl.semaphore_wait(barrier, cols + group - 2 + (cols - 1) * (subs - 1))

    def push(src, dst, send_sem, recv_sem, device):
        return pltpu.make_async_remote_copy(
            src_ref=src,
            dst_ref=dst,
            send_sem=send_sem,
            recv_sem=recv_sem,
            device_id=device,
            device_id_type=MESH,
        )

    def bound_copy(o, mine):
        p = across(o)
        n = r if mine else p
        return push(
            bounds.at[r], bounds.at[n], bound_sems.at[0, p], bound_sems.at[1, n], {"row": p}
        )

    def pair_copy(o, q, mine):
        p = beside(o)
        n = s if mine else p
        return push(
            pair_send.at[p, q],
            pair_recv.at[n, q],
            pair_sems.at[0, p, q],
            pair_sems.at[1, n, q],
            {"sub": p},
        )

    def image_copy(o, mine):
        p = along(o)
        n = z if mine else p
        return push(
            image_send.at[p],
            image_recv.at[n],
            image_sems.at[0, p],
            image_sems.at[1, n],
            {"col": p},
        )

    def dual_part(q, n):
        return dual_all.at[pl.ds((q * subs + n) * own_rb, own_rb)]

    def dual_copy(o, n, mine):
        p, m = along(o), beside(n)
        source = (z, s) if mine else (p, m)
        return push(
            dual_part(z, s),
            dual_part(*source),
            dual_sems.at[0, p, m],
            dual_sems.at[(1,) + source],
            {"col": p, "sub": m},
        )

    others = [(o, n) for o in range(cols - 1, -1, -1) for n in range(subs) if o or n]

    def gap_copy(o, mine):
        p = along(o)
        n = z if mine else p
        return push(
            gap_line.at[z], gap_line.at[n], gap_sems.at[0, p], gap_sems.at[1, n], {"col": p}
        )

    def group_copy(o, slot, mine):
        p, device = around(o)
        n = g if mine else p
        return push(
            gap_group.at[slot, g],
            gap_group.at[slot, n],
            group_sems.at[slot, 0, p],
            group_sems.at[slot, 1, n],
            device,
        )

    def adjoint_copy(o, slot, part, mine):
        p = across(o)
        n = r if mine else p
        span = pl.ds(part * chunk, chunk)
        return push(
            adjoint_send.at[span],
            adjoint_recv.at[slot, n, span],
            adjoint_sems.at[slot, 0, p, part],
            adjoint_sems.at[slot, 1, n, part],
            {"row": p},
        )

    for load in loads[:4]:
        load.wait()
    kind = kind_ref[...]
    bounds[r, 0] = vectors[0]
    bounds[r, 1] = jnp.where(kind == 2, -1e30, vectors[1])
    bounds[r, 2] = jnp.where(kind == 1, vectors[1] + vectors[2], 1e30)
    for o in range(1, rows):
        bound_copy(o, True).start()
    zero = jnp.zeros((16, 128), F32)
    none = jnp.zeros((16, 128), BF)
    sums[slots] = zero
    bar[col_blocks] = none
    dual_all[row_blocks] = none
    weight_ref[...] = jnp.ones((16, 128), F32)
    dual[...] = jnp.zeros_like(dual)
    dual_anchor[...] = jnp.zeros_like(dual)
    dual_total[...] = jnp.zeros_like(dual)
    loads[4].wait()
    loads[5].wait()

    def flip(i, unused):
        for u in range(16):
            k = i * 16 + u
            flipped[k] = blocks[index_ref[0, k]].T
        return unused

    lax.fori_loop(0, slots // 16, flip, 0)

    for o in range(1, rows):
        bound_copy(o, False).wait_recv()
    for o in range(1, rows):
        bound_copy(o, True).wait_send()

    for q in range(rows):
        for i in range(own_cb):
            j = q * own_cb + i
            new = -step_scale * bounds[q, 0, i : i + 1, :]
            new = jnp.minimum(
                jnp.maximum(new, bounds[q, 1, i : i + 1, :]), bounds[q, 2, i : i + 1, :]
            )
            new = jnp.broadcast_to(new, (16, 128))
            primal_new[j] = new
            bar[j] = (2.0 * new).astype(BF)
            primal[j] = zero
            primal_anchor[j] = zero
            primal_total[j] = zero

    def product(source, which, pair_of):
        def body(i, acc):
            for u in range(0, unroll, 2):
                k = i * unroll + u
                first = source[index_ref[2 * which + 1, k]]
                second = source[index_ref[2 * which + 1, k + 1]]
                left = jnp.concatenate(
                    [
                        jnp.concatenate([first, none], 1),
                        jnp.concatenate([none, second], 1),
                    ],
                    0,
                )
                parts = jnp.dot(left, pair_of(k), preferred_element_type=F32)
                acc = acc * same_ref[which, k] + parts[:16]
                sums[k] = acc
                acc = acc * same_ref[which, k + 1] + parts[16:]
                sums[k + 1] = acc
            return acc

        lax.fori_loop(0, slots // unroll, body, zero)

    def forward_pair(k):
        return jnp.concatenate([flipped[k], flipped[k + 1]], 0)

    def adjoint_pair(k):
        return jnp.concatenate([blocks[index_ref[2, k]], blocks[index_ref[2, k + 1]]], 0)

    def iteration(t, count):
        restart = flags_ref[t] == 1
        slot = lax.rem(t, 2)
        count = count + 1.0
        share = 1.0 / jnp.full((16, 128), count, F32)

        product(bar, 0, forward_pair)
        order = [along(o) for o in range(cols - 1, 0, -1)] + [z]
        for q in order:
            for o in range(1, subs):
                p = beside(o)
                for i in range(own_rb):
                    pair_send[p, q, i] = sums[last_row_ref[(q * subs + p) * own_rb + i]]
                pair_copy(o, q, True).start()

        def pair_sum(q):
            for o in range(1, subs):
                pair_copy(o, q, False).wait_recv()
            total = []
            for i in range(own_rb):
                value = sums[last_row_ref[(q * subs + s) * own_rb + i]]
                for o in range(1, subs):
                    value = value + pair_recv[beside(o), q, i]
                total.append(value)
            return total

        for o in range(cols - 1, 0, -1):
            q = along(o)
            total = pair_sum(q)
            for i in range(own_rb):
                image_send[q, i] = total[i].astype(BF)
            image_copy(o, True).start()
        image = pair_sum(z)

        def settle(j, gap):
            new = primal_new[j]
            total = primal_total[j] + new
            mean = total * share
            anchor = primal_anchor[j]
            primal[j] = jnp.where(restart, mean, new)
            primal_anchor[j] = jnp.where(restart, mean, anchor)
            primal_total[j] = jnp.where(restart, 0.0, total)
            away = mean - anchor
            return gap + away * away

        def settle_group(q):
            def four(i, gap):
                for u in range(4):
                    gap = settle(q * own_cb + i * 4 + u, gap)
                return gap

            return lax.fori_loop(0, own_cb // 4, four, zero)

        for o in range(1, rows):
            settle_group(across(o))
        gap_x = settle_group(r)

        for o in range(1, cols):
            image_copy(o, False).wait_recv()
            for i in range(own_rb):
                image[i] = image[i] + image_recv[along(o), i].astype(F32)
        gap_y = zero
        weight = weight_ref[...]
        for i in range(own_rb):
            demand = demand_ref[:, i * 128 : (i + 1) * 128]
            new = jnp.maximum(dual[i] + step_scale * weight * (demand - image[i]), 0.0)
            total = dual_total[i] + new
            mean = total * share
            anchor = dual_anchor[i]
            value = jnp.where(restart, mean, new)
            dual[i] = value
            dual_all[(z * subs + s) * own_rb + i] = value.astype(BF)
            dual_anchor[i] = jnp.where(restart, mean, anchor)
            dual_total[i] = jnp.where(restart, 0.0, total)
            away = mean - anchor
            gap_y = gap_y + away * away

        @pl.when(t < iters - 1)
        def _():
            for o, n in others:
                dual_copy(o, n, True).start()

            low = lax.broadcasted_iota(jnp.int32, (16, 128), 1) < 64
            gap_line[z] = jnp.where(
                low,
                gap_x + pltpu.roll(gap_x, 64, 1),
                gap_y + pltpu.roll(gap_y, 64, 1),
            )
            for o in range(cols - 1, 0, -1):
                gap_copy(o, True).start()

            for o, n in others:
                dual_copy(o, n, False).wait_recv()

            product(dual_all, 1, adjoint_pair)

            for o in range(1, cols):
                gap_copy(o, False).wait_recv()
            gap = gap_line[0]
            for p in range(1, cols):
                gap = gap + gap_line[p]
            gap_group[slot, g] = gap
            for o in range(1, group):
                group_copy(o, slot, True).start()

            for part in range(chunks):
                for u in range(chunk):
                    j = part * chunk + u
                    adjoint_send[j] = sums[last_col_ref[j]].astype(BF)
                for o in range(1, rows):
                    adjoint_copy(o, slot, part, True).start()

            for o in range(1, group):
                group_copy(o, slot, False).wait_recv()
            gap = gap_group[slot, 0]
            for p in range(1, group):
                gap = gap + gap_group[slot, p]
            sum_x = jnp.sum(jnp.where(low, gap, 0.0), axis=1, keepdims=True)
            sum_y = jnp.sum(jnp.where(low, 0.0, gap), axis=1, keepdims=True)
            sum_x = jnp.broadcast_to(sum_x, (16, 128))
            sum_y = jnp.broadcast_to(sum_y, (16, 128))
            ratio = jnp.sqrt((sum_y / total_rows + tiny) / (sum_x / total_cols + tiny))
            fresh = jnp.where(restart, jnp.sqrt(weight * ratio), weight)
            weight_ref[...] = fresh
            stride = step_scale / fresh

            for part in range(chunks):
                for o in range(1, rows):
                    adjoint_copy(o, slot, part, False).wait_recv()
                for u in range(chunk):
                    j = part * chunk + u
                    q, n = j // own_cb, j % own_cb
                    gradient = sums[last_col_ref[j]]
                    for o in range(1, rows):
                        gradient = gradient + adjoint_recv[slot, across(o), j].astype(F32)
                    old = primal[j]
                    new = old - stride * (bounds[q, 0, n : n + 1, :] - gradient)
                    new = jnp.maximum(new, bounds[q, 1, n : n + 1, :])
                    new = jnp.minimum(new, bounds[q, 2, n : n + 1, :])
                    primal_new[j] = new
                    bar[j] = (2.0 * new - old).astype(BF)

            for o in range(1, cols):
                gap_copy(o, True).wait_send()
            for o, n in others:
                dual_copy(o, n, True).wait_send()
            for o in range(1, group):
                group_copy(o, slot, True).wait_send()
            for o in range(1, rows):
                for part in range(chunks):
                    adjoint_copy(o, slot, part, True).wait_send()

        for o in range(1, cols):
            image_copy(o, True).wait_send()
        for o in range(1, subs):
            for q in order:
                pair_copy(o, q, True).wait_send()
        return jnp.where(restart, 0.0, count)

    lax.fori_loop(0, iters, iteration, jnp.zeros((), F32))
    for i in range(own_cb):
        primal_out[:, i * 128 : (i + 1) * 128] = primal[r * own_cb + i]
    for i in range(own_rb):
        dual_out[:, i * 128 : (i + 1) * 128] = dual[i]


def shards(
    rows,
    cols,
    subs,
    a_blocks,
    block_rows,
    block_cols,
    block_count,
    cost,
    lower,
    span,
    bound_kind,
    demand,
    restart_flags,
):
    blocks = a_blocks[0, 0]
    slots = blocks.shape[0]
    peers = cols * subs
    own_rb = demand.shape[1] // 128
    own_cb = cost.shape[0] // 128
    row_blocks = own_rb * peers
    col_blocks = own_cb * rows
    iters = restart_flags.shape[0]
    unroll = 96
    chunk = own_cb // 2
    live = jnp.arange(slots) < block_count[0, 0]
    row_list = block_rows[0, 0]
    col_list = block_cols[0, 0]
    slot_f, source_f, same_f, last_row = order_slots(
        row_list, col_list, live, row_blocks, col_blocks
    )
    slot_a, source_a, same_a, last_col = order_slots(
        col_list, row_list, live, col_blocks, row_blocks
    )
    index = jnp.stack([slot_f, source_f, slot_a, source_a])
    same = jnp.stack([same_f, same_a])
    sizes = (rows, cols, subs, iters, slots, own_rb, own_cb, unroll, chunk)
    smem = pl.BlockSpec(memory_space=pltpu.SMEM)
    vmem = pl.BlockSpec(memory_space=pltpu.VMEM)
    dma = pltpu.SemaphoreType.DMA
    tile = (16, 128)
    call = pl.pallas_call(
        functools.partial(kernel, sizes),
        out_shape=(
            jax.ShapeDtypeStruct((16, own_cb * 128), F32),
            jax.ShapeDtypeStruct((16, own_rb * 128), F32),
        ),
        in_specs=[smem] * 5 + [pl.BlockSpec(memory_space=pl.ANY)] * 6,
        out_specs=(vmem, vmem),
        scratch_shapes=[
            pltpu.VMEM((slots, 128, 128), BF),
            pltpu.VMEM((slots, 128, 128), BF),
            pltpu.VMEM((3, own_cb, 128), F32),
            pltpu.VMEM((own_cb, 128), jnp.int32),
            pltpu.VMEM((16, own_rb * 128), F32),
            pltpu.VMEM((slots + 1,) + tile, F32),
            pltpu.VMEM((col_blocks + 1,) + tile, BF),
            pltpu.VMEM((row_blocks + 1,) + tile, BF),
            pltpu.VMEM((rows, 3, own_cb, 128), F32),
            pltpu.VMEM((col_blocks,) + tile, F32),
            pltpu.VMEM((col_blocks,) + tile, F32),
            pltpu.VMEM((col_blocks,) + tile, F32),
            pltpu.VMEM((col_blocks,) + tile, F32),
            pltpu.VMEM((own_rb,) + tile, F32),
            pltpu.VMEM((own_rb,) + tile, F32),
            pltpu.VMEM((own_rb,) + tile, F32),
            pltpu.VMEM((subs, cols, own_rb) + tile, F32),
            pltpu.VMEM((subs, cols, own_rb) + tile, F32),
            pltpu.VMEM((cols, own_rb) + tile, BF),
            pltpu.VMEM((cols, own_rb) + tile, BF),
            pltpu.VMEM((col_blocks,) + tile, BF),
            pltpu.VMEM((2, rows, col_blocks) + tile, BF),
            pltpu.VMEM((cols,) + tile, F32),
            pltpu.VMEM((2, rows * subs) + tile, F32),
            pltpu.VMEM(tile, F32),
            dma((6,)),
            dma((2, rows)),
            dma((2, subs, cols)),
            dma((2, cols)),
            dma((2, cols, subs)),
            dma((2, cols)),
            dma((2, 2, rows * subs)),
            dma((2, 2, rows, col_blocks // chunk)),
        ],
        compiler_params=pltpu.CompilerParams(
            collective_id=0,
            has_side_effects=True,
            vmem_limit_bytes=60 * 1024 * 1024,
        ),
    )
    as_blocks = lambda v: v.reshape(own_cb, 128)
    return call(
        index,
        same,
        last_row,
        last_col,
        restart_flags,
        blocks,
        as_blocks(cost),
        as_blocks(lower),
        as_blocks(span),
        as_blocks(bound_kind),
        demand,
    )


def solution(mesh):
    placed = (
        P(("inst", "row"), ("col", "sub"), None, None, None),
        P(("inst", "row"), ("col", "sub"), None),
        P(("inst", "row"), ("col", "sub"), None),
        P(("inst", "row"), ("col", "sub")),
        P(("inst", "row", "col", "sub")),
        P(("inst", "row", "col", "sub")),
        P(("inst", "row", "col", "sub")),
        P(("inst", "row", "col", "sub")),
        P(None, ("inst", "row", "col", "sub")),
        P(),
    )
    shape = mesh.shape
    return jax.shard_map(
        functools.partial(shards, shape["row"], shape["col"], shape["sub"]),
        mesh=mesh,
        in_specs=placed,
        out_specs=(P(None, ("inst", "row", "col", "sub")), P(None, ("inst", "row", "col", "sub"))),
        check_vma=False,
    )
```

```python
import functools

import jax
import jax.numpy as jnp
from jax import lax
from jax.experimental import pallas as pl
from jax.experimental.pallas import tpu as pltpu
from jax.sharding import PartitionSpec as P

step_scale = 0.8
tiny = 1e-06
MESH = pl.DeviceIdType.MESH
BF = jnp.bfloat16
F32 = jnp.float32


def order_slots(key, source, live, groups, dead_source):
    slots = key.shape[0]
    places = jnp.arange(slots, dtype=jnp.int32)
    key = jnp.where(live, key, groups)
    source = jnp.where(live, source, dead_source)
    ahead = (key[None, :] < key[:, None]) | (
        (key[None, :] == key[:, None]) & (places[None, :] < places[:, None])
    )
    rank = jnp.sum(ahead.astype(jnp.int32), axis=1)
    hit = rank[None, :] == places[:, None]
    slot = jnp.sum(jnp.where(hit, places[None, :], 0), axis=1)
    sorted_key = jnp.sum(jnp.where(hit, key[None, :], 0), axis=1)
    sorted_source = jnp.sum(jnp.where(hit, source[None, :], 0), axis=1)
    before = jnp.concatenate([jnp.full((1,), -1, jnp.int32), sorted_key[:-1]])
    same = (before == sorted_key).astype(F32)
    names = jnp.arange(groups, dtype=jnp.int32)
    upto = jnp.sum((key[None, :] <= names[:, None]).astype(jnp.int32), axis=1)
    own = jnp.sum((key[None, :] == names[:, None]).astype(jnp.int32), axis=1)
    last = jnp.where(own > 0, upto - 1, slots)
    return slot, sorted_source, same, last


def kernel(
    sizes,
    index_ref,
    same_ref,
    last_row_ref,
    last_col_ref,
    flags_ref,
    blocks_hbm,
    cost_hbm,
    lower_hbm,
    span_hbm,
    kind_hbm,
    demand_hbm,
    primal_out,
    dual_out,
    blocks,
    flipped,
    vectors,
    kind_ref,
    demand_ref,
    sums,
    bar,
    dual_all,
    bounds,
    primal,
    primal_new,
    primal_anchor,
    primal_total,
    dual,
    dual_anchor,
    dual_total,
    pair_send,
    pair_recv,
    image_send,
    image_recv,
    adjoint_send,
    adjoint_recv,
    gap_line,
    gap_group,
    weight_ref,
    copy_sems,
    bound_sems,
    pair_sems,
    image_sems,
    dual_sems,
    forward_sems,
    gap_sems,
    group_sems,
    adjoint_sems,
):
    rows, cols, subs, iters, slots, own_rb, own_cb, unroll, chunk = sizes
    group = rows * subs
    row_blocks = own_rb * cols * subs
    col_blocks = own_cb * rows
    chunks = col_blocks // chunk
    total_rows = own_rb * 128 * rows * cols * subs
    total_cols = own_cb * 128 * rows * cols * subs
    r = lax.axis_index("row")
    z = lax.axis_index("col")
    s = lax.axis_index("sub")
    g = r * subs + s

    loads = [
        pltpu.make_async_copy(cost_hbm, vectors.at[0], copy_sems.at[0]),
        pltpu.make_async_copy(lower_hbm, vectors.at[1], copy_sems.at[1]),
        pltpu.make_async_copy(span_hbm, vectors.at[2], copy_sems.at[2]),
        pltpu.make_async_copy(kind_hbm, kind_ref, copy_sems.at[3]),
        pltpu.make_async_copy(demand_hbm, demand_ref, copy_sems.at[4]),
        pltpu.make_async_copy(blocks_hbm, blocks, copy_sems.at[5]),
    ]
    for load in loads:
        load.start()

    def along(o):
        if cols & (cols - 1):
            return lax.rem(z + o, cols)
        p = z
        bit = 1
        while bit < cols:
            if o & bit:
                p = p + bit * (1 - 2 * lax.rem(lax.div(z, bit), 2))
            bit *= 2
        return p

    def across(o):
        return lax.rem(r + o, rows)

    def beside(o):
        return lax.rem(s + o, subs)

    def around(o):
        p = lax.rem(g + o, group)
        return p, {"row": lax.div(p, subs), "sub": lax.rem(p, subs)}

    barrier = pltpu.get_barrier_semaphore()
    for o in range(1, cols):
        pl.semaphore_signal(barrier, inc=1, device_id={"col": along(o)}, device_id_type=MESH)
    for o in range(1, group):
        pl.semaphore_signal(barrier, inc=1, device_id=around(o)[1], device_id_type=MESH)
    pl.semaphore_wait(barrier, cols + group - 2)

    def push(src, dst, send_sem, recv_sem, device):
        return pltpu.make_async_remote_copy(
            src_ref=src,
            dst_ref=dst,
            send_sem=send_sem,
            recv_sem=recv_sem,
            device_id=device,
            device_id_type=MESH,
        )

    def bound_copy(o, mine):
        p = across(o)
        n = r if mine else p
        return push(
            bounds.at[r], bounds.at[n], bound_sems.at[0, p], bound_sems.at[1, n], {"row": p}
        )

    def pair_copy(o, q, mine):
        p = beside(o)
        n = s if mine else p
        return push(
            pair_send.at[p, q],
            pair_recv.at[n, q],
            pair_sems.at[0, p, q],
            pair_sems.at[1, n, q],
            {"sub": p},
        )

    def image_copy(o, mine):
        p = along(o)
        n = z if mine else p
        return push(
            image_send.at[p],
            image_recv.at[n],
            image_sems.at[0, p],
            image_sems.at[1, n],
            {"col": p},
        )

    def dual_part(q, n):
        return dual_all.at[pl.ds((q * subs + n) * own_rb, own_rb)]

    def dual_copy(o, mine):
        p = along(o)
        n = z if mine else p
        return push(
            dual_part(z, s), dual_part(n, s), dual_sems.at[0, p], dual_sems.at[1, n], {"col": p}
        )

    def forward_copy(o, q, mine):
        p = beside(o)
        n = s if mine else p
        return push(
            dual_part(q, s),
            dual_part(q, n),
            forward_sems.at[0, p, q],
            forward_sems.at[1, n, q],
            {"sub": p},
        )

    def gap_copy(o, mine):
        p = along(o)
        n = z if mine else p
        return push(
            gap_line.at[z], gap_line.at[n], gap_sems.at[0, p], gap_sems.at[1, n], {"col": p}
        )

    def group_copy(o, slot, mine):
        p, device = around(o)
        n = g if mine else p
        return push(
            gap_group.at[slot, g],
            gap_group.at[slot, n],
            group_sems.at[slot, 0, p],
            group_sems.at[slot, 1, n],
            device,
        )

    def adjoint_copy(o, slot, part, mine):
        p = across(o)
        n = r if mine else p
        span = pl.ds(part * chunk, chunk)
        return push(
            adjoint_send.at[span],
            adjoint_recv.at[slot, n, span],
            adjoint_sems.at[slot, 0, p, part],
            adjoint_sems.at[slot, 1, n, part],
            {"row": p},
        )

    for load in loads[:4]:
        load.wait()
    kind = kind_ref[...]
    bounds[r, 0] = vectors[0]
    bounds[r, 1] = jnp.where(kind == 2, -1e30, vectors[1])
    bounds[r, 2] = jnp.where(kind == 1, vectors[1] + vectors[2], 1e30)
    for o in range(1, rows):
        bound_copy(o, True).start()
    zero = jnp.zeros((16, 128), F32)
    none = jnp.zeros((16, 128), BF)
    sums[slots] = zero
    bar[col_blocks] = none
    dual_all[row_blocks] = none
    weight_ref[...] = jnp.ones((16, 128), F32)
    dual[...] = jnp.zeros_like(dual)
    dual_anchor[...] = jnp.zeros_like(dual)
    dual_total[...] = jnp.zeros_like(dual)
    loads[4].wait()
    loads[5].wait()

    def flip(i, unused):
        for u in range(16):
            k = i * 16 + u
            flipped[k] = blocks[index_ref[0, k]].T
        return unused

    lax.fori_loop(0, slots // 16, flip, 0)

    for o in range(1, rows):
        bound_copy(o, False).wait_recv()
    for o in range(1, rows):
        bound_copy(o, True).wait_send()

    for q in range(rows):
        for i in range(own_cb):
            j = q * own_cb + i
            new = -step_scale * bounds[q, 0, i : i + 1, :]
            new = jnp.minimum(
                jnp.maximum(new, bounds[q, 1, i : i + 1, :]), bounds[q, 2, i : i + 1, :]
            )
            new = jnp.broadcast_to(new, (16, 128))
            primal_new[j] = new
            bar[j] = (2.0 * new).astype(BF)
            primal[j] = zero
            primal_anchor[j] = zero
            primal_total[j] = zero

    def product(source, which, pair_of):
        def body(i, acc):
            for u in range(0, unroll, 2):
                k = i * unroll + u
                first = source[index_ref[2 * which + 1, k]]
                second = source[index_ref[2 * which + 1, k + 1]]
                left = jnp.concatenate(
                    [
                        jnp.concatenate([first, none], 1),
                        jnp.concatenate([none, second], 1),
                    ],
                    0,
                )
                parts = jnp.dot(left, pair_of(k), preferred_element_type=F32)
                acc = acc * same_ref[which, k] + parts[:16]
                sums[k] = acc
                acc = acc * same_ref[which, k + 1] + parts[16:]
                sums[k + 1] = acc
            return acc

        lax.fori_loop(0, slots // unroll, body, zero)

    def forward_pair(k):
        return jnp.concatenate([flipped[k], flipped[k + 1]], 0)

    def adjoint_pair(k):
        return jnp.concatenate([blocks[index_ref[2, k]], blocks[index_ref[2, k + 1]]], 0)

    def iteration(t, count):
        restart = flags_ref[t] == 1
        slot = lax.rem(t, 2)
        count = count + 1.0
        share = 1.0 / jnp.full((16, 128), count, F32)

        product(bar, 0, forward_pair)
        order = [along(o) for o in range(cols - 1, 0, -1)] + [z]
        for q in order:
            for o in range(1, subs):
                p = beside(o)
                for i in range(own_rb):
                    pair_send[p, q, i] = sums[last_row_ref[(q * subs + p) * own_rb + i]]
                pair_copy(o, q, True).start()

        def pair_sum(q):
            for o in range(1, subs):
                pair_copy(o, q, False).wait_recv()
            total = []
            for i in range(own_rb):
                value = sums[last_row_ref[(q * subs + s) * own_rb + i]]
                for o in range(1, subs):
                    value = value + pair_recv[beside(o), q, i]
                total.append(value)
            return total

        for o in range(cols - 1, 0, -1):
            q = along(o)
            total = pair_sum(q)
            for i in range(own_rb):
                image_send[q, i] = total[i].astype(BF)
            image_copy(o, True).start()
        image = pair_sum(z)

        def settle(j, gap):
            new = primal_new[j]
            total = primal_total[j] + new
            mean = total * share
            anchor = primal_anchor[j]
            primal[j] = jnp.where(restart, mean, new)
            primal_anchor[j] = jnp.where(restart, mean, anchor)
            primal_total[j] = jnp.where(restart, 0.0, total)
            away = mean - anchor
            return gap + away * away

        def settle_group(q):
            def four(i, gap):
                for u in range(4):
                    gap = settle(q * own_cb + i * 4 + u, gap)
                return gap

            return lax.fori_loop(0, own_cb // 4, four, zero)

        for o in range(1, rows):
            settle_group(across(o))
        gap_x = settle_group(r)

        for o in range(1, cols):
            image_copy(o, False).wait_recv()
            for i in range(own_rb):
                image[i] = image[i] + image_recv[along(o), i].astype(F32)
        gap_y = zero
        weight = weight_ref[...]
        for i in range(own_rb):
            demand = demand_ref[:, i * 128 : (i + 1) * 128]
            new = jnp.maximum(dual[i] + step_scale * weight * (demand - image[i]), 0.0)
            total = dual_total[i] + new
            mean = total * share
            anchor = dual_anchor[i]
            value = jnp.where(restart, mean, new)
            dual[i] = value
            dual_all[(z * subs + s) * own_rb + i] = value.astype(BF)
            dual_anchor[i] = jnp.where(restart, mean, anchor)
            dual_total[i] = jnp.where(restart, 0.0, total)
            away = mean - anchor
            gap_y = gap_y + away * away

        @pl.when(t < iters - 1)
        def _():
            for o in range(cols - 1, 0, -1):
                dual_copy(o, True).start()
            for o in range(1, subs):
                forward_copy(o, z, True).start()

            low = lax.broadcasted_iota(jnp.int32, (16, 128), 1) < 64
            gap_line[z] = jnp.where(
                low,
                gap_x + pltpu.roll(gap_x, 64, 1),
                gap_y + pltpu.roll(gap_y, 64, 1),
            )
            for o in range(cols - 1, 0, -1):
                gap_copy(o, True).start()

            for o in range(1, cols):
                dual_copy(o, False).wait_recv()
                for n in range(1, subs):
                    forward_copy(n, along(o), True).start()
            for o in range(cols):
                for n in range(1, subs):
                    forward_copy(n, along(o), False).wait_recv()

            product(dual_all, 1, adjoint_pair)

            for o in range(1, cols):
                gap_copy(o, False).wait_recv()
            gap = gap_line[0]
            for p in range(1, cols):
                gap = gap + gap_line[p]
            gap_group[slot, g] = gap
            for o in range(1, group):
                group_copy(o, slot, True).start()

            for part in range(chunks):
                for u in range(chunk):
                    j = part * chunk + u
                    adjoint_send[j] = sums[last_col_ref[j]].astype(BF)
                for o in range(1, rows):
                    adjoint_copy(o, slot, part, True).start()

            for o in range(1, group):
                group_copy(o, slot, False).wait_recv()
            gap = gap_group[slot, 0]
            for p in range(1, group):
                gap = gap + gap_group[slot, p]
            sum_x = jnp.sum(jnp.where(low, gap, 0.0), axis=1, keepdims=True)
            sum_y = jnp.sum(jnp.where(low, 0.0, gap), axis=1, keepdims=True)
            sum_x = jnp.broadcast_to(sum_x, (16, 128))
            sum_y = jnp.broadcast_to(sum_y, (16, 128))
            ratio = jnp.sqrt((sum_y / total_rows + tiny) / (sum_x / total_cols + tiny))
            fresh = jnp.where(restart, jnp.sqrt(weight * ratio), weight)
            weight_ref[...] = fresh
            stride = step_scale / fresh

            for part in range(chunks):
                for o in range(1, rows):
                    adjoint_copy(o, slot, part, False).wait_recv()
                for u in range(chunk):
                    j = part * chunk + u
                    q, n = j // own_cb, j % own_cb
                    gradient = sums[last_col_ref[j]]
                    for o in range(1, rows):
                        gradient = gradient + adjoint_recv[slot, across(o), j].astype(F32)
                    old = primal[j]
                    new = old - stride * (bounds[q, 0, n : n + 1, :] - gradient)
                    new = jnp.maximum(new, bounds[q, 1, n : n + 1, :])
                    new = jnp.minimum(new, bounds[q, 2, n : n + 1, :])
                    primal_new[j] = new
                    bar[j] = (2.0 * new - old).astype(BF)

            for o in range(1, cols):
                dual_copy(o, True).wait_send()
                gap_copy(o, True).wait_send()
            for o in range(1, subs):
                for q in order:
                    forward_copy(o, q, True).wait_send()
            for o in range(1, group):
                group_copy(o, slot, True).wait_send()
            for o in range(1, rows):
                for part in range(chunks):
                    adjoint_copy(o, slot, part, True).wait_send()

        for o in range(1, cols):
            image_copy(o, True).wait_send()
        for o in range(1, subs):
            for q in order:
                pair_copy(o, q, True).wait_send()
        return jnp.where(restart, 0.0, count)

    lax.fori_loop(0, iters, iteration, jnp.zeros((), F32))
    for i in range(own_cb):
        primal_out[:, i * 128 : (i + 1) * 128] = primal[r * own_cb + i]
    for i in range(own_rb):
        dual_out[:, i * 128 : (i + 1) * 128] = dual[i]


def shards(
    rows,
    cols,
    subs,
    a_blocks,
    block_rows,
    block_cols,
    block_count,
    cost,
    lower,
    span,
    bound_kind,
    demand,
    restart_flags,
):
    blocks = a_blocks[0, 0]
    slots = blocks.shape[0]
    peers = cols * subs
    own_rb = demand.shape[1] // 128
    own_cb = cost.shape[0] // 128
    row_blocks = own_rb * peers
    col_blocks = own_cb * rows
    iters = restart_flags.shape[0]
    unroll = slots
    chunk = own_cb // 2
    live = jnp.arange(slots) < block_count[0, 0]
    row_list = block_rows[0, 0]
    col_list = block_cols[0, 0]
    slot_f, source_f, same_f, last_row = order_slots(
        row_list, col_list, live, row_blocks, col_blocks
    )
    slot_a, source_a, same_a, last_col = order_slots(
        col_list, row_list, live, col_blocks, row_blocks
    )
    index = jnp.stack([slot_f, source_f, slot_a, source_a])
    same = jnp.stack([same_f, same_a])
    sizes = (rows, cols, subs, iters, slots, own_rb, own_cb, unroll, chunk)
    smem = pl.BlockSpec(memory_space=pltpu.SMEM)
    vmem = pl.BlockSpec(memory_space=pltpu.VMEM)
    dma = pltpu.SemaphoreType.DMA
    tile = (16, 128)
    call = pl.pallas_call(
        functools.partial(kernel, sizes),
        out_shape=(
            jax.ShapeDtypeStruct((16, own_cb * 128), F32),
            jax.ShapeDtypeStruct((16, own_rb * 128), F32),
        ),
        in_specs=[smem] * 5 + [pl.BlockSpec(memory_space=pl.ANY)] * 6,
        out_specs=(vmem, vmem),
        scratch_shapes=[
            pltpu.VMEM((slots, 128, 128), BF),
            pltpu.VMEM((slots, 128, 128), BF),
            pltpu.VMEM((3, own_cb, 128), F32),
            pltpu.VMEM((own_cb, 128), jnp.int32),
            pltpu.VMEM((16, own_rb * 128), F32),
            pltpu.VMEM((slots + 1,) + tile, F32),
            pltpu.VMEM((col_blocks + 1,) + tile, BF),
            pltpu.VMEM((row_blocks + 1,) + tile, BF),
            pltpu.VMEM((rows, 3, own_cb, 128), F32),
            pltpu.VMEM((col_blocks,) + tile, F32),
            pltpu.VMEM((col_blocks,) + tile, F32),
            pltpu.VMEM((col_blocks,) + tile, F32),
            pltpu.VMEM((col_blocks,) + tile, F32),
            pltpu.VMEM((own_rb,) + tile, F32),
            pltpu.VMEM((own_rb,) + tile, F32),
            pltpu.VMEM((own_rb,) + tile, F32),
            pltpu.VMEM((subs, cols, own_rb) + tile, F32),
            pltpu.VMEM((subs, cols, own_rb) + tile, F32),
            pltpu.VMEM((cols, own_rb) + tile, BF),
            pltpu.VMEM((cols, own_rb) + tile, BF),
            pltpu.VMEM((col_blocks,) + tile, BF),
            pltpu.VMEM((2, rows, col_blocks) + tile, BF),
            pltpu.VMEM((cols,) + tile, F32),
            pltpu.VMEM((2, rows * subs) + tile, F32),
            pltpu.VMEM(tile, F32),
            dma((6,)),
            dma((2, rows)),
            dma((2, subs, cols)),
            dma((2, cols)),
            dma((2, cols)),
            dma((2, subs, cols)),
            dma((2, cols)),
            dma((2, 2, rows * subs)),
            dma((2, 2, rows, col_blocks // chunk)),
        ],
        compiler_params=pltpu.CompilerParams(
            collective_id=0,
            has_side_effects=True,
            vmem_limit_bytes=60 * 1024 * 1024,
        ),
    )
    as_blocks = lambda v: v.reshape(own_cb, 128)
    return call(
        index,
        same,
        last_row,
        last_col,
        restart_flags,
        blocks,
        as_blocks(cost),
        as_blocks(lower),
        as_blocks(span),
        as_blocks(bound_kind),
        demand,
    )


def solution(mesh):
    placed = (
        P(("inst", "row"), ("col", "sub"), None, None, None),
        P(("inst", "row"), ("col", "sub"), None),
        P(("inst", "row"), ("col", "sub"), None),
        P(("inst", "row"), ("col", "sub")),
        P(("inst", "row", "col", "sub")),
        P(("inst", "row", "col", "sub")),
        P(("inst", "row", "col", "sub")),
        P(("inst", "row", "col", "sub")),
        P(None, ("inst", "row", "col", "sub")),
        P(),
    )
    shape = mesh.shape
    return jax.shard_map(
        functools.partial(shards, shape["row"], shape["col"], shape["sub"]),
        mesh=mesh,
        in_specs=placed,
        out_specs=(P(None, ("inst", "row", "col", "sub")), P(None, ("inst", "row", "col", "sub"))),
        check_vma=False,
    )
```
